256 devices in a mesh: clip: 8 (over z), blk: 8 (over y_hi, x), head: 4 (over y_lo, core).
Axes of the slice: x: 4, y: 4 (y_hi: 2, y_lo: 2; y = y_hi * 2 + y_lo), z: 8, core: 2. Of those that a mesh axis runs over, the one named last changes fastest.
Arguments:
- q_in: bfloat16 [32768, 2560], P(('clip', 'blk', 'head')), parts along dimension 0, may hold values from -4 to 4
- k_in: bfloat16 [32768, 2560], P(('clip', 'blk', 'head')), parts along dimension 0, may hold values from -4 to 4
- v_in: bfloat16 [32768, 2560], P(('clip', 'blk', 'head')), parts along dimension 0, may hold values from -6 to 6
- q_gain: float32 [2560], replicated, may hold values from 0.5 to 2
- k_gain: float32 [2560], replicated, may hold values from 0.5 to 2
- out_weight: bfloat16 [2560, 5120], P('head'), may hold values from -0.125 to 0.125
- out_bias: float32 [5120], replicated, may hold values from -3 to 3
- out_gate: float32 [5120], replicated, may hold values from -4 to 4
Outputs:
- branch_out: bfloat16 [32768, 5120], P(('clip', 'blk', 'head')), parts along dimension 0
The draws below stay inside these ranges and needn't reach their ends.
There are 8 independent parts, one for each index of `clip`. The reference program is written for one: setup_inputs(seed, part) draws one part's arguments, and reference() takes and returns one part's arrays. A program takes and returns all parts, laid end to end along the dimension named above; an argument that names none is the same for every part. Nothing has to cross between parts.
All inputs are finite; a program needn't handle non-finite values.
Results may differ from the reference program's by a relative error of at most 0.008.
Values may be sent and summed in bfloat16 or wider, within the bound.
A program may use at most 128 MiB of HBM per device.

```python
import math
import jax
import jax.numpy as jnp
from jax import lax

D = 5120
HD = 128
HEADS = 20
TOKENS = 4096


def draw_q_in(key, part):
    key = jax.random.fold_in(key, 1)
    return jnp.clip(jax.random.normal(key, (TOKENS, HEADS * HD), jnp.float32), -4.0, 4.0).astype(jnp.bfloat16)


def draw_k_in(key, part):
    key = jax.random.fold_in(key, 2)
    return jnp.clip(jax.random.normal(key, (TOKENS, HEADS * HD), jnp.float32), -4.0, 4.0).astype(jnp.bfloat16)


def block_levels(own_key, dims, cuts, low, top_value):
    loudness = 1.0
    for dim, parts in cuts:
        draws = jax.random.uniform(jax.random.fold_in(jax.random.fold_in(own_key, 6), dim), (parts,), jnp.float32, low / len(cuts), top_value / len(cuts))
        loudness = loudness * jnp.repeat(jnp.exp(draws), dims[dim] // parts).reshape((-1,) + (1,) * (len(dims) - 1 - dim))
    return loudness


def centred(rng, shape, width, bound, cuts=(), kind=jnp.bfloat16):
    values = width * jax.random.normal(rng, shape, jnp.float32)
    if cuts:
        values = values * block_levels(rng, shape, cuts, -0.22, 0.18)
    return jnp.clip(values, -bound, bound).astype(kind)


def setup_inputs(seed: int = 0, part: int = 0) -> dict:
    splits = jax.random.split(jax.random.key(seed), 9)
    part_splits = jax.random.split(jax.random.fold_in(splits[8], part), 9)
    q_in = draw_q_in(jax.random.fold_in(jax.random.fold_in(splits[8], part), 71), part)
    k_in = draw_k_in(jax.random.fold_in(jax.random.fold_in(splits[8], part), 71), part)
    v_in = centred(part_splits[2], (TOKENS, HEADS * HD), 1.0, 6.0, ((0, 32),))
    q_gain = jnp.clip(jnp.exp(jax.random.uniform(splits[3], (HEADS * HD,), jnp.float32, math.log(0.5), math.log(2.0))), 0.5, 2.0)
    k_gain = jnp.clip(jnp.exp(jax.random.uniform(splits[4], (HEADS * HD,), jnp.float32, math.log(0.5), math.log(2.0))), 0.5, 2.0)
    out_weight = centred(splits[5], (HEADS * HD, D), (HEADS * HD) ** -0.5, 0.125, ((0, 4),))
    out_bias = centred(splits[6], (D,), 0.5, 3.0, (), jnp.float32)
    out_gate = centred(splits[7], (D,), 1.0, 4.0, (), jnp.float32)
    return dict(q_in=q_in, k_in=k_in, v_in=v_in, q_gain=q_gain, k_gain=k_gain, out_weight=out_weight, out_bias=out_bias, out_gate=out_gate)


def normalize(values, gain):
    wide = values.astype(jnp.float32)
    factor = lax.rsqrt(lax.optimization_barrier(jnp.mean(wide * wide, axis=-1, keepdims=True)) + 1e-06)
    return (wide * factor * gain).astype(jnp.bfloat16)

def one_head(triple):
    query_head, key_head, value_head = triple
    scores = jnp.dot(query_head, key_head.T, preferred_element_type=jnp.float32) * HD ** (-0.5)
    highest = lax.optimization_barrier(jnp.max(scores, axis=1, keepdims=True))
    weights = jnp.exp(scores - highest)
    summed = lax.optimization_barrier(jnp.sum(weights, axis=1, keepdims=True))
    mixed = jnp.dot(weights.astype(jnp.bfloat16), value_head, preferred_element_type=jnp.float32)
    return (mixed / summed).astype(jnp.bfloat16)

def reference(q_in, k_in, v_in, q_gain, k_gain, out_weight, out_bias, out_gate):
    length = q_in.shape[0]
    queries = normalize(q_in, q_gain).reshape(length, HEADS, HD).transpose(1, 0, 2)
    keys = normalize(k_in, k_gain).reshape(length, HEADS, HD).transpose(1, 0, 2)
    values = v_in.reshape(length, HEADS, HD).transpose(1, 0, 2)
    attended = lax.map(one_head, (queries, keys, values))
    attended = attended.transpose(1, 0, 2).reshape(length, HEADS * HD)
    projected = jnp.dot(attended, out_weight, preferred_element_type=jnp.float32) + out_bias
    return (out_gate * projected).astype(jnp.bfloat16)
```

```python
import functools
import math

import jax
import jax.numpy as jnp
from jax import lax
from jax.experimental import pallas as pl
from jax.experimental.pallas import tpu as pltpu
from jax.sharding import PartitionSpec as P

HD = 128
SIDE = 4
CHIPS = SIDE * SIDE
CLASS_HEADS = 10
HEADS = 20
KEY_CHUNK = 512
OUT_CHUNK = 512
MESH = pl.DeviceIdType.MESH


def kernel(
    q_ref, k_ref, v_ref, qg_ref, kg_ref, w_ref, bias_ref, gate_ref, out_ref,
    stage, qkv, scores, mixed, attended, weight, own, part_out, part_in,
    local_sem, full_send, full_recv, left_send, left_recv, row_send, row_recv,
    pair_send, pair_recv, pair_left_send, pair_left_recv, w_send, w_recv,
    mix_send, mix_recv, part_send, part_recv,
):
    tile = q_ref.shape[0]
    half = tile // 2
    keys = 2 * CHIPS * tile
    width = out_ref.shape[1]
    blk, head = lax.axis_index("blk"), lax.axis_index("head")
    x, core = lax.rem(blk, SIDE), lax.rem(head, 2)
    y = 2 * (blk // SIDE) + head // 2

    def chip(dy, dx):
        return lax.rem(y + dy, SIDE), lax.rem(x + dx, SIDE)

    def device(dy, dx):
        yy, xx = chip(dy, dx)
        return {"blk": (yy // 2) * SIDE + xx, "head": lax.rem(yy, 2) * 2 + core}

    sibling = {"blk": blk, "head": (head // 2) * 2 + 1 - core}

    def full_head(yy, xx):
        return CLASS_HEADS * lax.rem(yy, 2) + SIDE * (yy // 2) + xx

    def left_head(yy):
        return CLASS_HEADS * lax.rem(yy, 2) + 2 * SIDE + yy // 2

    def rows(start, size):
        return pl.ds(pl.multiple_of(start, half), size)

    def remote(src, dst, send, recv, target):
        return pltpu.make_async_remote_copy(
            src_ref=src, dst_ref=dst, send_sem=send, recv_sem=recv,
            device_id=target, device_id_type=MESH,
        )

    own_weight = pltpu.make_async_copy(w_ref, weight.at[core], local_sem.at[2])
    own_weight.start()

    barrier = pltpu.get_barrier_semaphore()

    def greet(r, carry):
        pl.semaphore_signal(
            barrier, inc=1, device_id=device(r // SIDE, lax.rem(r, SIDE)), device_id_type=MESH
        )
        return carry

    lax.fori_loop(1, CHIPS, greet, 0)
    pl.semaphore_signal(barrier, inc=1, device_id=sibling, device_id_type=MESH)

    def normalize(ref, gain_ref, which, scale):
        wide = ref[...].astype(jnp.float32)
        factor = lax.rsqrt(jnp.mean(wide * wide, axis=-1, keepdims=True) + 1e-06)
        for h in range(HEADS):
            cols = slice(h * HD, (h + 1) * HD)
            gain = gain_ref[:, cols] * scale if scale is not None else gain_ref[:, cols]
            stage[which, h] = (ref[:, cols].astype(jnp.float32) * factor * gain).astype(jnp.bfloat16)

    normalize(q_ref, qg_ref, 0, HD ** (-0.5) * math.log2(math.e))
    normalize(k_ref, kg_ref, 1, None)
    for h in range(HEADS):
        stage[2, h] = v_ref[:, h * HD : (h + 1) * HD]

    pl.semaphore_wait(barrier, CHIPS)

    w_copy = remote(w_ref, weight.at[core], w_send, w_recv, sibling)
    w_copy.start()

    def left_copy(dy):
        yy, xx = chip(dy, 0)
        return remote(
            stage.at[:, left_head(yy)], qkv.at[1, :, rows(dy * tile, tile), :],
            left_send.at[dy], left_recv.at[dy], device(dy, 0),
        )

    def full_copy(r):
        dy, dx = r // SIDE, lax.rem(r, SIDE)
        yy, xx = chip(dy, dx)
        return remote(
            stage.at[:, full_head(yy, xx)], qkv.at[0, :, rows(r * tile, tile), :],
            full_send.at[r], full_recv.at[r], device(dy, dx),
        )

    def pair_copy(r):
        here = qkv.at[0, pl.ds(1, 2), rows(r * tile, tile), :]
        there = qkv.at[0, pl.ds(1, 2), rows((CHIPS + r) * tile, tile), :]
        return remote(here, there, pair_send.at[r], pair_recv.at[r], sibling)

    def row_copy(dx):
        here = qkv.at[1, pl.ds(1, 2), rows(0, SIDE * tile), :]
        there = qkv.at[1, pl.ds(1, 2), rows(dx * SIDE * tile, SIDE * tile), :]
        return remote(here, there, row_send.at[dx], row_recv.at[dx], device(0, dx))

    def pair_left_copy(dx):
        here = qkv.at[1, pl.ds(1, 2), rows(dx * SIDE * tile, SIDE * tile), :]
        there = qkv.at[1, pl.ds(1, 2), rows((CHIPS + dx * SIDE) * tile, SIDE * tile), :]
        return remote(here, there, pair_left_send.at[dx], pair_left_recv.at[dx], sibling)

    def over(first, last, act):
        def step(i, carry):
            act(i)
            return carry

        lax.fori_loop(first, last, step, 0)

    over(1, SIDE, lambda dy: left_copy(dy).start())
    over(1, CHIPS, lambda r: full_copy(r).start())
    own_full = pltpu.make_async_copy(
        stage.at[:, full_head(y, x)], qkv.at[0, :, pl.ds(0, tile), :], local_sem.at[0]
    )
    own_left = pltpu.make_async_copy(
        stage.at[:, left_head(y)], qkv.at[1, :, pl.ds(0, tile), :], local_sem.at[1]
    )
    own_full.start()
    own_left.start()
    own_full.wait()
    own_left.wait()
    pair_copy(0).start()

    over(1, SIDE, lambda dy: left_copy(dy).wait_recv())
    over(1, SIDE, lambda dx: row_copy(dx).start())
    pair_left_copy(0).start()

    def pass_on(r):
        full_copy(r).wait_recv()
        pair_copy(r).start()

    over(1, CHIPS, pass_on)

    def pass_on_left(dx):
        row_copy(dx).wait_recv()
        pair_left_copy(dx).start()

    over(1, SIDE, pass_on_left)
    over(0, CHIPS, lambda r: pair_copy(r).wait_recv())
    over(0, SIDE, lambda dx: pair_left_copy(dx).wait_recv())

    def mix_copy(b):
        is_left = b // (2 * SIDE)
        t = b - 2 * SIDE * is_left
        ey = jnp.where(is_left == 1, 2 * t, 2 * (t // SIDE))
        dx = jnp.where(is_left == 1, 0, lax.rem(t, SIDE))
        slot = jnp.where(is_left == 1, 2 * SIDE + y // 2, SIDE * (y // 2) + x)
        lanes = pl.ds(pl.multiple_of(slot * HD, HD), HD)
        return remote(
            mixed.at[b], attended.at[:, lanes], mix_send.at[b], mix_recv.at[b], device(ey, dx)
        ), lanes

    def attend(b):
        is_left = b // (2 * SIDE)
        t = b - 2 * SIDE * is_left
        ey = jnp.where(is_left == 1, 2 * t, 2 * (t // SIDE))
        dx = jnp.where(is_left == 1, 0, lax.rem(SIDE - lax.rem(t, SIDE), SIDE))

        def at(dy):
            dy = lax.rem(dy, SIDE)
            return jnp.where(is_left == 1, dy, dy * SIDE + dx) * tile

        q = jnp.concatenate(
            [
                qkv[is_left, 0, rows(at(2 * SIDE - ey), tile), :],
                qkv[is_left, 0, rows(at(2 * SIDE - ey - 1) + half, half), :],
                qkv[is_left, 0, rows(at(2 * SIDE - ey + 1), half), :],
            ],
            axis=0,
        )
        chunk = min(KEY_CHUNK, keys)
        highest = jnp.full((2 * tile, HD), -jnp.inf, jnp.float32)
        for c in range(keys // chunk):
            s = lax.dot_general(
                q, qkv[is_left, 1, pl.ds(c * chunk, chunk), :], (((1,), (1,)), ((), ())),
                preferred_element_type=jnp.float32,
            )
            scores[:, c * chunk : (c + 1) * chunk] = s
            for g in range(chunk // HD):
                highest = jnp.maximum(highest, s[:, g * HD : (g + 1) * HD])
        top = jnp.max(highest, axis=1, keepdims=True)
        summed = jnp.zeros((2 * tile, HD), jnp.float32)
        total = jnp.zeros((2 * tile, HD), jnp.float32)
        for c in range(keys // chunk):
            p = jnp.exp2(scores[:, c * chunk : (c + 1) * chunk] - top)
            for g in range(chunk // HD):
                summed = summed + p[:, g * HD : (g + 1) * HD]
            total = total + jnp.dot(
                p.astype(jnp.bfloat16), qkv[is_left, 2, pl.ds(c * chunk, chunk), :],
                preferred_element_type=jnp.float32,
            )
        mixed[b] = (total / jnp.sum(summed, axis=1, keepdims=True)).astype(jnp.bfloat16)

    def attend_send(b):
        attend(b)
        mix_copy(b)[0].start()

    over(1, 2 * SIDE, attend_send)
    attend_send(2 * SIDE + 1)

    def attend_here(b):
        attend(b)
        attended[:, mix_copy(b)[1]] = mixed[b]

    def here(i):
        attend_here(i * 2 * SIDE)

    over(0, 2, here)

    over(1, 2 * SIDE, lambda b: mix_copy(b)[0].wait_recv())
    mix_copy(2 * SIDE + 1)[0].wait_recv()
    own_weight.wait()
    w_copy.wait_recv()

    wide_chunk = min(OUT_CHUNK, width)
    chunks = width // wide_chunk

    def cols_of(j):
        return pl.ds(pl.multiple_of(j * wide_chunk, HD), wide_chunk)

    def part_copy(d, j):
        here = part_out.at[pl.ds(d * half, half), cols_of(j)]
        there = part_in.at[pl.ds((1 - d) * half, half), cols_of(j)]
        return remote(
            here, there, part_send.at[d, j], part_recv.at[d, j], device(1 if d == 0 else SIDE - 1, 0)
        )

    depth = weight.shape[1]

    def project(j):
        cols = cols_of(j)
        r = jnp.dot(attended[:, :depth], weight[0, :, cols], preferred_element_type=jnp.float32)
        r = r + jnp.dot(attended[:, depth:], weight[1, :, cols], preferred_element_type=jnp.float32)
        part_out[:, cols] = r[tile:].astype(jnp.bfloat16)
        part_copy(0, j).start()
        part_copy(1, j).start()
        own[:, cols] = r[:tile]

    over(0, chunks, project)

    def finish(j):
        cols = cols_of(j)
        part_copy(0, j).wait_recv()
        part_copy(1, j).wait_recv()
        total = own[:, cols] + part_in[:, cols].astype(jnp.float32) + bias_ref[:, cols]
        out_ref[:, cols] = (gate_ref[:, cols] * total).astype(jnp.bfloat16)

    over(0, chunks, finish)

    over(1, SIDE, lambda dy: left_copy(dy).wait_send())
    over(1, CHIPS, lambda r: full_copy(r).wait_send())
    over(0, CHIPS, lambda r: pair_copy(r).wait_send())
    over(1, SIDE, lambda dx: row_copy(dx).wait_send())
    over(0, SIDE, lambda dx: pair_left_copy(dx).wait_send())
    w_copy.wait_send()
    over(1, 2 * SIDE, lambda b: mix_copy(b)[0].wait_send())
    mix_copy(2 * SIDE + 1)[0].wait_send()

    def sent(j):
        part_copy(0, j).wait_send()
        part_copy(1, j).wait_send()

    over(0, chunks, sent)


def body(q_in, k_in, v_in, q_gain, k_gain, out_weight, out_bias, out_gate):
    tile = q_in.shape[0]
    depth, width = out_weight.shape
    keys = 2 * CHIPS * tile
    chunks = width // min(OUT_CHUNK, width)
    vmem = pl.BlockSpec(memory_space=pltpu.VMEM)
    dma = pltpu.SemaphoreType.DMA
    return pl.pallas_call(
        kernel,
        out_shape=jax.ShapeDtypeStruct((tile, width), jnp.bfloat16),
        in_specs=[vmem] * 5 + [pl.BlockSpec(memory_space=pl.ANY)] + [vmem] * 2,
        out_specs=vmem,
        scratch_shapes=[
            pltpu.VMEM((3, HEADS, tile, HD), jnp.bfloat16),
            pltpu.VMEM((2, 3, keys, HD), jnp.bfloat16),
            pltpu.VMEM((2 * tile, keys), jnp.float32),
            pltpu.VMEM((CLASS_HEADS, 2 * tile, HD), jnp.bfloat16),
            pltpu.VMEM((2 * tile, CLASS_HEADS * HD), jnp.bfloat16),
            pltpu.VMEM((2, depth, width), jnp.bfloat16),
            pltpu.VMEM((tile, width), jnp.float32),
            pltpu.VMEM((tile, width), jnp.bfloat16),
            pltpu.VMEM((tile, width), jnp.bfloat16),
            dma((3,)),
            dma((CHIPS,)), dma((CHIPS,)),
            dma((SIDE,)), dma((SIDE,)),
            dma((SIDE,)), dma((SIDE,)),
            dma((CHIPS,)), dma((CHIPS,)),
            dma((SIDE,)), dma((SIDE,)),
            dma, dma,
            dma((CLASS_HEADS,)), dma((CLASS_HEADS,)),
            dma((2, chunks)), dma((2, chunks)),
        ],
        compiler_params=pltpu.CompilerParams(
            collective_id=0, has_side_effects=True, vmem_limit_bytes=60 * 1024 * 1024
        ),
        name="attention_branch",
    )(
        q_in, k_in, v_in, q_gain.reshape(1, -1), k_gain.reshape(1, -1), out_weight,
        out_bias.reshape(1, -1), out_gate.reshape(1, -1),
    )


def solution(mesh):
    split = P(("clip", "blk", "head"), None)
    in_specs = (split, split, split, P(), P(), P("head", None), P(), P())
    return jax.shard_map(body, mesh=mesh, in_specs=in_specs, out_specs=split, check_vma=False)
```

```python
import functools
import math

import jax
import jax.numpy as jnp
from jax import lax
from jax.experimental import pallas as pl
from jax.experimental.pallas import tpu as pltpu
from jax.sharding import PartitionSpec as P

HD = 128
SIDE = 4
CHIPS = SIDE * SIDE
CLASS_HEADS = 10
HEADS = 20
KEY_CHUNK = 512
OUT_CHUNK = 512
MESH = pl.DeviceIdType.MESH


def kernel(
    q_ref, k_ref, v_ref, qg_ref, kg_ref, w_ref, bias_ref, gate_ref, out_ref,
    stage, qkv, scores, mixed, attended, weight, own, part_out, part_in,
    local_sem, full_send, full_recv, left_send, left_recv, row_send, row_recv, relay_send, relay_recv,
    pair_send, pair_recv, pair_left_send, pair_left_recv, w_send, w_recv,
    mix_send, mix_recv, part_send, part_recv,
):
    tile = q_ref.shape[0]
    half = tile // 2
    keys = 2 * CHIPS * tile
    width = out_ref.shape[1]
    blk, head = lax.axis_index("blk"), lax.axis_index("head")
    x, core = lax.rem(blk, SIDE), lax.rem(head, 2)
    y = 2 * (blk // SIDE) + head // 2

    def chip(dy, dx):
        return lax.rem(y + dy, SIDE), lax.rem(x + dx, SIDE)

    def device(dy, dx):
        yy, xx = chip(dy, dx)
        return {"blk": (yy // 2) * SIDE + xx, "head": lax.rem(yy, 2) * 2 + core}

    sibling = {"blk": blk, "head": (head // 2) * 2 + 1 - core}

    def full_head(yy, xx):
        return CLASS_HEADS * lax.rem(yy, 2) + SIDE * (yy // 2) + xx

    def left_head(yy):
        return CLASS_HEADS * lax.rem(yy, 2) + 2 * SIDE + yy // 2

    def rows(start, size):
        return pl.ds(pl.multiple_of(start, half), size)

    def remote(src, dst, send, recv, target):
        return pltpu.make_async_remote_copy(
            src_ref=src, dst_ref=dst, send_sem=send, recv_sem=recv,
            device_id=target, device_id_type=MESH,
        )

    own_weight = pltpu.make_async_copy(w_ref, weight.at[core], local_sem.at[2])
    own_weight.start()

    barrier = pltpu.get_barrier_semaphore()

    def greet(r, carry):
        pl.semaphore_signal(
            barrier, inc=1, device_id=device(r // SIDE, lax.rem(r, SIDE)), device_id_type=MESH
        )
        return carry

    lax.fori_loop(1, CHIPS, greet, 0)
    pl.semaphore_signal(barrier, inc=1, device_id=sibling, device_id_type=MESH)

    def normalize(ref, gain_ref, which, scale):
        wide = ref[...].astype(jnp.float32)
        factor = lax.rsqrt(jnp.mean(wide * wide, axis=-1, keepdims=True) + 1e-06)
        for h in range(HEADS):
            cols = slice(h * HD, (h + 1) * HD)
            gain = gain_ref[cols].reshape(1, HD)
            if scale is not None:
                gain = gain * scale
            stage[which, h] = (ref[:, cols].astype(jnp.float32) * factor * gain).astype(jnp.bfloat16)

    normalize(q_ref, qg_ref, 0, HD ** (-0.5) * math.log2(math.e))
    normalize(k_ref, kg_ref, 1, None)
    for h in range(HEADS):
        stage[2, h] = v_ref[:, h * HD : (h + 1) * HD]

    pl.semaphore_wait(barrier, CHIPS)

    w_copy = remote(w_ref, weight.at[core], w_send, w_recv, sibling)
    w_copy.start()

    def left_copy(dy):
        yy, xx = chip(dy, 0)
        return remote(
            stage.at[:, left_head(yy)], qkv.at[1, :, rows(dy * tile, tile), :],
            left_send.at[dy], left_recv.at[dy], device(dy, 0),
        )

    def full_copy(r):
        dy, dx = r // SIDE, lax.rem(r, SIDE)
        yy, xx = chip(dy, dx)
        return remote(
            stage.at[:, full_head(yy, xx)], qkv.at[0, :, rows(r * tile, tile), :],
            full_send.at[r], full_recv.at[r], device(dy, dx),
        )

    def pair_copy(r):
        here = qkv.at[0, pl.ds(1, 2), rows(r * tile, tile), :]
        there = qkv.at[0, pl.ds(1, 2), rows((CHIPS + r) * tile, tile), :]
        return remote(here, there, pair_send.at[r], pair_recv.at[r], sibling)

    def left_rows(i):
        return qkv.at[1, pl.ds(1, 2), rows(i * tile, tile), :]

    def row_copy(d, t):
        dx = 1 + 2 * d
        return remote(
            left_rows(t), left_rows(dx * SIDE + t), row_send.at[d, t], row_recv.at[d, t], device(0, dx)
        )

    def relay_copy(t):
        dx = 1 + 2 * (t // 2)
        return remote(
            left_rows(dx * SIDE + t), left_rows(2 * SIDE + t), relay_send.at[t], relay_recv.at[t],
            device(0, dx),
        )

    def pair_left_copy(i):
        return remote(
            left_rows(i), left_rows(CHIPS + i), pair_left_send.at[i], pair_left_recv.at[i], sibling
        )

    def over(first, last, act):
        def step(i, carry):
            act(i)
            return carry

        lax.fori_loop(first, last, step, 0)

    over(1, CHIPS, lambda r: full_copy(r).start())
    over(1, SIDE, lambda dy: left_copy(dy).start())
    own_full = pltpu.make_async_copy(
        stage.at[:, full_head(y, x)], qkv.at[0, :, pl.ds(0, tile), :], local_sem.at[0]
    )
    own_left = pltpu.make_async_copy(
        stage.at[:, left_head(y)], qkv.at[1, :, pl.ds(0, tile), :], local_sem.at[1]
    )
    own_full.start()
    own_left.start()
    own_full.wait()
    own_left.wait()
    pair_copy(0).start()

    def pass_on(r):
        full_copy(r).wait_recv()
        pair_copy(r).start()

    over(1, CHIPS, pass_on)

    def spread_left(t):
        row_copy(0, t).start()
        row_copy(1, t).start()
        pair_left_copy(t).start()

    spread_left(0)
    over(0, CHIPS, lambda r: pair_copy(r).wait_recv())

    def target(is_left, u, i):
        if is_left:
            return 2 * i, 0, 2 * SIDE + i, 2 * SIDE + y // 2
        ey, dx = 2 * (u // 2), 2 * lax.rem(u, 2) + i
        return ey, dx, (ey // 2) * SIDE + dx, SIDE * (y // 2) + x

    def mix_place(is_left, slot, rnd):
        lanes = pl.ds(pl.multiple_of(slot * HD, HD), HD)
        return pl.ds((1 - rnd) * tile, tile), lanes

    def mix_copy(rnd, is_left, u, i):
        ey, dx, t, slot = target(is_left, u, i)
        place = mix_place(is_left, slot, rnd)
        return remote(
            mixed.at[rnd, t], attended.at[place[0], place[1]], mix_send.at[rnd, t], mix_recv.at[rnd, t],
            device(ey, dx),
        )

    def attend(rnd, is_left, u):
        which = 1 if is_left else 0
        pieces = []
        for i in range(2):
            ey, dx, _, _ = target(is_left, u, i)

            def at(dy):
                dy = lax.rem(dy, SIDE)
                return (dy if is_left else dy * SIDE + lax.rem(SIDE - dx, SIDE)) * tile

            if rnd == 0:
                pieces += [
                    qkv[which, 0, rows(at(2 * SIDE - ey - 1) + half, half), :],
                    qkv[which, 0, rows(at(2 * SIDE - ey + 1), half), :],
                ]
            else:
                pieces.append(qkv[which, 0, rows(at(2 * SIDE - ey), tile), :])
        q = jnp.concatenate(pieces, axis=0)
        chunk = min(KEY_CHUNK, keys)
        highest = jnp.full((2 * tile, HD), -jnp.inf, jnp.float32)
        for c in range(keys // chunk):
            s = lax.dot_general(
                q, qkv[which, 1, pl.ds(c * chunk, chunk), :], (((1,), (1,)), ((), ())),
                preferred_element_type=jnp.float32,
            )
            scores[:, c * chunk : (c + 1) * chunk] = s
            for g in range(chunk // HD):
                highest = jnp.maximum(highest, s[:, g * HD : (g + 1) * HD])
        top = jnp.max(highest, axis=1, keepdims=True)
        summed = jnp.zeros((2 * tile, HD), jnp.float32)
        total = jnp.zeros((2 * tile, HD), jnp.float32)
        for c in range(keys // chunk):
            p = jnp.exp2(scores[:, c * chunk : (c + 1) * chunk] - top)
            for g in range(chunk // HD):
                summed = summed + p[:, g * HD : (g + 1) * HD]
            total = total + jnp.dot(
                p.astype(jnp.bfloat16), qkv[which, 2, pl.ds(c * chunk, chunk), :],
                preferred_element_type=jnp.float32,
            )
        result = (total / jnp.sum(summed, axis=1, keepdims=True)).astype(jnp.bfloat16)
        for i in range(2):
            _, _, t, slot = target(is_left, u, i)
            mixed[rnd, t] = result[i * tile : (i + 1) * tile]

        def keep():
            place = mix_place(is_left, target(is_left, u, 0)[3], rnd)
            attended[place[0], place[1]] = result[:tile]

        if is_left:
            keep()
        else:
            pl.when(u == 0)(keep)
            pl.when(u > 0)(lambda: mix_copy(rnd, is_left, u, 0).start())
        mix_copy(rnd, is_left, u, 1).start()

    def first_round(u):
        attend(0, False, u)

        @pl.when(u > 0)
        def _():
            left_copy(u).wait_recv()
            spread_left(u)

    over(0, SIDE, first_round)

    def second_round(u):
        row_copy(0, u).wait_recv()
        row_copy(1, u).wait_recv()
        relay_copy(u).start()
        pair_left_copy(SIDE + u).start()
        pair_left_copy(3 * SIDE + u).start()
        attend(1, False, u)

    over(0, SIDE, second_round)

    def end_left(t):
        relay_copy(t).wait_recv()
        pair_left_copy(2 * SIDE + t).start()

    over(0, SIDE, end_left)
    over(0, CHIPS, lambda i: pair_left_copy(i).wait_recv())
    own_weight.wait()
    w_copy.wait_recv()

    def mix_wait(rnd):
        def full(u):
            pl.when(u > 0)(lambda: mix_copy(rnd, False, u, 0).wait_recv())
            mix_copy(rnd, False, u, 1).wait_recv()

        over(0, SIDE, full)
        mix_copy(rnd, True, 0, 1).wait_recv()

    wide_chunk = min(OUT_CHUNK, width)
    chunks = width // wide_chunk

    def cols_of(j):
        return pl.ds(pl.multiple_of(j * wide_chunk, HD), wide_chunk)

    def part_copy(d, j):
        here = part_out.at[pl.ds(d * half, half), cols_of(j)]
        there = part_in.at[pl.ds((1 - d) * half, half), cols_of(j)]
        return remote(
            here, there, part_send.at[d, j], part_recv.at[d, j], device(1 if d == 0 else SIDE - 1, 0)
        )

    depth = weight.shape[1]

    def product(at, cols):
        r = jnp.dot(attended[at, :depth], weight[0, :, cols], preferred_element_type=jnp.float32)
        return r + jnp.dot(attended[at, depth:], weight[1, :, cols], preferred_element_type=jnp.float32)

    def project_sent(j):
        cols = cols_of(j)
        part_out[:, cols] = product(pl.ds(tile, tile), cols).astype(jnp.bfloat16)
        part_copy(0, j).start()
        part_copy(1, j).start()

    def project_kept(j):
        cols = cols_of(j)
        own[:, cols] = product(pl.ds(0, tile), cols)

    attend(0, True, 0)
    attend(1, True, 0)
    mix_wait(0)
    over(0, chunks, project_sent)
    mix_wait(1)
    over(0, chunks, project_kept)

    def finish(j):
        cols = cols_of(j)
        part_copy(0, j).wait_recv()
        part_copy(1, j).wait_recv()
        total = own[:, cols] + part_in[:, cols].astype(jnp.float32) + bias_ref[:, cols]
        out_ref[:, cols] = (gate_ref[:, cols] * total).astype(jnp.bfloat16)

    over(0, chunks, finish)

    over(1, SIDE, lambda dy: left_copy(dy).wait_send())
    over(1, CHIPS, lambda r: full_copy(r).wait_send())
    over(0, CHIPS, lambda r: pair_copy(r).wait_send())

    def row_sent(t):
        row_copy(0, t).wait_send()
        row_copy(1, t).wait_send()
        relay_copy(t).wait_send()

    over(0, SIDE, row_sent)
    over(0, CHIPS, lambda i: pair_left_copy(i).wait_send())
    w_copy.wait_send()
    for rnd in range(2):

        def mix_sent(u, rnd=rnd):
            pl.when(u > 0)(lambda: mix_copy(rnd, False, u, 0).wait_send())
            mix_copy(rnd, False, u, 1).wait_send()

        over(0, SIDE, mix_sent)
        mix_copy(rnd, True, 0, 1).wait_send()

    def sent(j):
        part_copy(0, j).wait_send()
        part_copy(1, j).wait_send()

    over(0, chunks, sent)


def body(q_in, k_in, v_in, q_gain, k_gain, out_weight, out_bias, out_gate):
    tile = q_in.shape[0]
    depth, width = out_weight.shape
    keys = 2 * CHIPS * tile
    chunks = width // min(OUT_CHUNK, width)
    vmem = pl.BlockSpec(memory_space=pltpu.VMEM)
    dma = pltpu.SemaphoreType.DMA
    return pl.pallas_call(
        kernel,
        out_shape=pltpu.VMEM((tile, width), jnp.bfloat16),
        in_specs=[vmem] * 5 + [pl.BlockSpec(memory_space=pl.ANY)] + [vmem] * 2,
        out_specs=vmem,
        scratch_shapes=[
            pltpu.VMEM((3, HEADS, tile, HD), jnp.bfloat16),
            pltpu.VMEM((2, 3, keys, HD), jnp.bfloat16),
            pltpu.VMEM((2 * tile, keys), jnp.float32),
            pltpu.VMEM((2, CLASS_HEADS, tile, HD), jnp.bfloat16),
            pltpu.VMEM((2 * tile, CLASS_HEADS * HD), jnp.bfloat16),
            pltpu.VMEM((2, depth, width), jnp.bfloat16),
            pltpu.VMEM((tile, width), jnp.float32),
            pltpu.VMEM((tile, width), jnp.bfloat16),
            pltpu.VMEM((tile, width), jnp.bfloat16),
            dma((3,)),
            dma((CHIPS,)), dma((CHIPS,)),
            dma((SIDE,)), dma((SIDE,)),
            dma((2, SIDE)), dma((2, SIDE)),
            dma((SIDE,)), dma((SIDE,)),
            dma((CHIPS,)), dma((CHIPS,)),
            dma((CHIPS,)), dma((CHIPS,)),
            dma, dma,
            dma((2, CLASS_HEADS)), dma((2, CLASS_HEADS)),
            dma((2, chunks)), dma((2, chunks)),
        ],
        compiler_params=pltpu.CompilerParams(
            collective_id=0, has_side_effects=True, vmem_limit_bytes=60 * 1024 * 1024
        ),
        name="attention_branch",
    )(
        q_in, k_in, v_in, q_gain, k_gain, out_weight,
        out_bias.reshape(1, -1), out_gate.reshape(1, -1),
    )


def solution(mesh):
    split = P(("clip", "blk", "head"), None)
    in_specs = (split, split, split, P(), P(), P("head", None), P(), P())
    return jax.shard_map(body, mesh=mesh, in_specs=in_specs, out_specs=split, check_vma=False)
```

```python
import functools
import math

import jax
import jax.numpy as jnp
from jax import lax
from jax.experimental import pallas as pl
from jax.experimental.pallas import tpu as pltpu
from jax.sharding import PartitionSpec as P

HD = 128
SIDE = 4
CHIPS = SIDE * SIDE
CLASS_HEADS = 10
HEADS = 20
KEY_CHUNK = 512
OUT_CHUNK = 1024
MESH = pl.DeviceIdType.MESH


def hops(r):
    dy, dx = r // SIDE, r % SIDE
    return min(dy, SIDE - dy) + min(dx, SIDE - dx)


FAR = sorted(range(1, CHIPS), key=lambda r: -hops(r))
LATE = [r for r in FAR if r // SIDE % 2 == 0]


def kernel(
    q_ref, k_ref, v_ref, qg_ref, kg_ref, w_ref, bias_ref, gate_ref, out_ref,
    stage, qkv, scores, mixed, attended, left_mixed, left_attended, weight, other, own, part_out, part_in,
    local_sem, full_send, full_recv, late_send, late_recv, left_send, left_recv, row_send, row_recv, relay_send, relay_recv,
    pair_send, pair_recv, pair_left_send, pair_left_recv, w_send, w_recv,
    near_send, near_recv, ring_send, ring_recv, other_send, other_recv, left_mix_send, left_mix_recv,
    mix_send, mix_recv, part_send, part_recv,
):
    tile = q_ref.shape[0]
    half = tile // 2
    keys = 2 * CHIPS * tile
    width = out_ref.shape[1]
    blk, head, z = lax.axis_index("blk"), lax.axis_index("head"), lax.axis_index("clip")
    clips = lax.axis_size("clip")
    depth = w_ref.shape[0]
    left_row = 2 * SIDE * HD - depth
    piece = HD // clips
    x, core = lax.rem(blk, SIDE), lax.rem(head, 2)
    y = 2 * (blk // SIDE) + head // 2

    def chip(dy, dx):
        return lax.rem(y + dy, SIDE), lax.rem(x + dx, SIDE)

    def device(dy, dx):
        yy, xx = chip(dy, dx)
        return {"blk": (yy // 2) * SIDE + xx, "head": lax.rem(yy, 2) * 2 + core}

    sibling = {"blk": blk, "head": (head // 2) * 2 + 1 - core}

    def full_head(yy, xx):
        return CLASS_HEADS * lax.rem(yy, 2) + SIDE * (yy // 2) + xx

    def left_head(yy):
        return CLASS_HEADS * lax.rem(yy, 2) + 2 * SIDE + yy // 2

    def rows(start, size):
        return pl.ds(pl.multiple_of(start, half), size)

    def remote(src, dst, send, recv, target):
        return pltpu.make_async_remote_copy(
            src_ref=src, dst_ref=dst, send_sem=send, recv_sem=recv,
            device_id=target, device_id_type=MESH,
        )

    own_weight = pltpu.make_async_copy(w_ref, weight.at[core], local_sem.at[2])
    own_weight.start()

    barrier = pltpu.get_barrier_semaphore()

    def greet(r, carry):
        pl.semaphore_signal(
            barrier, inc=1, device_id=device(r // SIDE, lax.rem(r, SIDE)), device_id_type=MESH
        )
        return carry

    lax.fori_loop(1, CHIPS, greet, 0)

    def clip_at(dz):
        return {"clip": lax.rem(z + dz, clips), "blk": blk, "head": head}

    beside = [1, clips - 1] if clips > 2 else [1][: clips - 1]
    for dz in beside:
        pl.semaphore_signal(barrier, inc=1, device_id=clip_at(dz), device_id_type=MESH)
    pl.semaphore_signal(barrier, inc=1, device_id=sibling, device_id_type=MESH)

    def normalize(ref, gain_ref, which, scale):
        wide = ref[...].astype(jnp.float32)
        factor = lax.rsqrt(jnp.mean(wide * wide, axis=-1, keepdims=True) + 1e-06)
        for h in range(HEADS):
            cols = slice(h * HD, (h + 1) * HD)
            gain = gain_ref[cols].reshape(1, HD)
            if scale is not None:
                gain = gain * scale
            stage[which, h] = (ref[:, cols].astype(jnp.float32) * factor * gain).astype(jnp.bfloat16)

    normalize(q_ref, qg_ref, 0, HD ** (-0.5) * math.log2(math.e))
    normalize(k_ref, kg_ref, 1, None)
    for h in range(HEADS):
        stage[2, h] = v_ref[:, h * HD : (h + 1) * HD].T

    pl.semaphore_wait(barrier, CHIPS + len(beside))

    w_copy = remote(w_ref, weight.at[core], w_send, w_recv, sibling)
    w_copy.start()

    def near_copy(d):
        start = z * 2 * piece + d * piece
        return remote(
            w_ref.at[pl.ds(pl.multiple_of(left_row + start, piece), piece)],
            other.at[pl.ds(pl.multiple_of(start, piece), piece)],
            near_send.at[d], near_recv.at[d], device(1 + 2 * d, 0),
        )

    def slice_of(origin):
        return other.at[pl.ds(pl.multiple_of(origin * 2 * piece, 2 * piece), 2 * piece)]

    def origin_of(d, step):
        return lax.rem(z + (clips - step if d == 0 else step), clips)

    def ring_copy(d, step):
        moved = slice_of(origin_of(d, step - 1))
        return remote(
            moved, moved, ring_send.at[d, step], ring_recv.at[d, step], clip_at(1 if d == 0 else clips - 1)
        )

    def other_copy(origin):
        return remote(
            slice_of(origin), slice_of(origin), other_send.at[origin], other_recv.at[origin], sibling
        )

    ring_steps = [clips // 2, (clips - 1) // 2]

    def ring(step):
        @pl.when(core == 1)
        def _():
            if step == 1:
                near_copy(0).wait_recv()
                near_copy(1).wait_recv()
                other_copy(z).start()
            for d in range(2):
                if 1 < step <= ring_steps[d] + 1:
                    ring_copy(d, step - 1).wait_recv()
                    other_copy(origin_of(d, step - 1)).start()
                if step <= ring_steps[d]:
                    ring_copy(d, step).start()

    def left_copy(dy):
        yy, xx = chip(dy, 0)
        return remote(
            stage.at[:, left_head(yy)], qkv.at[1, :, rows(dy * tile, tile), :],
            left_send.at[dy], left_recv.at[dy], device(dy, 0),
        )

    def full_copy(r):
        dy, dx = r // SIDE, r % SIDE
        first = 1 if dy % 2 == 0 else 0
        return remote(
            stage.at[pl.ds(first, 3 - first), full_head(*chip(dy, dx))],
            qkv.at[0, pl.ds(first, 3 - first), rows(r * tile, tile), :],
            full_send.at[r], full_recv.at[r], device(dy, dx),
        )

    def late_copy(r):
        dy, dx = r // SIDE, r % SIDE
        return remote(
            stage.at[0, full_head(*chip(dy, dx))], qkv.at[0, 0, rows(r * tile, tile), :],
            late_send.at[r], late_recv.at[r], device(dy, dx),
        )

    def pair_copy(r):
        here = qkv.at[0, pl.ds(1, 2), rows(r * tile, tile), :]
        there = qkv.at[0, pl.ds(1, 2), rows((CHIPS + r) * tile, tile), :]
        return remote(here, there, pair_send.at[r], pair_recv.at[r], sibling)

    def left_rows(i):
        return qkv.at[1, pl.ds(1, 2), rows(i * tile, tile), :]

    def row_copy(d, t):
        dx = 1 + 2 * d
        return remote(
            left_rows(t), left_rows(dx * SIDE + t), row_send.at[d, t], row_recv.at[d, t], device(0, dx)
        )

    def relay_copy(t):
        dx = 1 + 2 * (t // 2)
        return remote(
            left_rows(dx * SIDE + t), left_rows(2 * SIDE + t), relay_send.at[t], relay_recv.at[t],
            device(0, dx),
        )

    def pair_left_copy(i):
        return remote(
            left_rows(i), left_rows(CHIPS + i), pair_left_send.at[i], pair_left_recv.at[i], sibling
        )

    def over(first, last, act):
        def step(i, carry):
            act(i)
            return carry

        lax.fori_loop(first, last, step, 0)

    @pl.when(core == 1)
    def _():
        near_copy(0).start()
        near_copy(1).start()

    for r in FAR:
        full_copy(r).start()
    over(1, SIDE, lambda dy: left_copy(dy).start())
    for r in LATE:
        late_copy(r).start()
    own_full = pltpu.make_async_copy(
        stage.at[:, full_head(y, x)], qkv.at[0, :, pl.ds(0, tile), :], local_sem.at[0]
    )
    own_left = pltpu.make_async_copy(
        stage.at[:, left_head(y)], qkv.at[1, :, pl.ds(0, tile), :], local_sem.at[1]
    )
    own_full.start()
    own_left.start()
    own_full.wait()
    own_left.wait()
    pair_copy(0).start()

    def pass_on(r):
        full_copy(r).wait_recv()
        pair_copy(r).start()

    for r in FAR:
        pass_on(r)

    def spread_left(t):
        row_copy(0, t).start()
        row_copy(1, t).start()
        pair_left_copy(t).start()

    spread_left(0)
    over(0, CHIPS, lambda r: pair_copy(r).wait_recv())

    def softmax_rows(which, q):
        count = q.shape[0]
        chunk = min(KEY_CHUNK, keys)
        highest = jnp.full((8, count), -jnp.inf, jnp.float32)
        for c in range(keys // chunk):
            s = lax.dot_general(
                qkv[which, 1, pl.ds(c * chunk, chunk), :], q, (((1,), (1,)), ((), ())),
                preferred_element_type=jnp.float32,
            )
            scores[c * chunk : (c + 1) * chunk, :] = s
            highest = jnp.maximum(highest, jnp.max(s.reshape(chunk // 8, 8, count), axis=0))
        top = jnp.max(highest, axis=0, keepdims=True)
        summed = jnp.zeros((8, count), jnp.float32)
        total = jnp.zeros((HD, count), jnp.float32)
        for c in range(keys // chunk):
            p = jnp.exp2(scores[c * chunk : (c + 1) * chunk, :] - top)
            summed = summed + jnp.sum(p.reshape(chunk // 8, 8, count), axis=0)
            values = jnp.concatenate(
                [qkv[which, 2, pl.ds(k * tile, tile), :] for k in range(c * chunk // tile, (c + 1) * chunk // tile)],
                axis=1,
            )
            total = total + jnp.dot(values, p.astype(jnp.bfloat16), preferred_element_type=jnp.float32)
        return (total / jnp.sum(summed, axis=0, keepdims=True)).T.astype(jnp.bfloat16)

    def lanes_of(slot):
        return pl.ds(pl.multiple_of(slot * HD, HD), HD)

    def mix_place(rnd):
        return pl.ds((1 - rnd) * tile, tile), lanes_of(SIDE * (y // 2) + x)

    def mix_copy(rnd, ey, dx):
        place, t = mix_place(rnd), (ey // 2) * SIDE + dx
        return remote(
            mixed.at[rnd, t], attended.at[place[0], place[1]], mix_send.at[rnd, t], mix_recv.at[rnd, t],
            device(ey, dx),
        )

    def attend(rnd, ey):
        pieces = []
        for dx in range(SIDE):

            def at(dy):
                return (lax.rem(dy, SIDE) * SIDE + (SIDE - dx) % SIDE) * tile

            if rnd == 0:
                pieces += [
                    qkv[0, 0, rows(at(2 * SIDE - ey - 1) + half, half), :],
                    qkv[0, 0, rows(at(2 * SIDE - ey + 1), half), :],
                ]
            else:
                pieces.append(qkv[0, 0, rows(at(2 * SIDE - ey), tile), :])
        result = softmax_rows(0, jnp.concatenate(pieces, axis=0))
        for dx in range(SIDE):
            mixed[rnd, (ey // 2) * SIDE + dx] = result[dx * tile : (dx + 1) * tile]

        @pl.when(ey == 0)
        def _():
            place = mix_place(rnd)
            attended[place[0], place[1]] = result[:tile]

        pl.when(ey > 0)(lambda: mix_copy(rnd, ey, 0).start())
        for dx in (2, 1, 3):
            mix_copy(rnd, ey, dx).start()

    def left_place(dy):
        return lanes_of(y // 2 + 2 * (dy & 1 if isinstance(dy, int) else lax.rem(dy, 2)))

    def left_mix_copy(dy):
        return remote(
            left_mixed.at[dy], left_attended.at[:, left_place(dy)], left_mix_send.at[dy],
            left_mix_recv.at[dy], device(SIDE - dy, 0),
        )

    def attend_left():
        result = softmax_rows(1, qkv[1, 0, pl.ds(0, SIDE * tile), :])
        left_attended[:, left_place(0)] = result[:tile]
        for dy in (2, 1, 3):
            left_mixed[dy] = result[dy * tile : (dy + 1) * tile]
            left_mix_copy(dy).start()

    def mix_wait(rnd):
        def full(t):
            mix_copy(rnd, 2 * (t // SIDE), lax.rem(t, SIDE)).wait_recv()

        over(1, 2 * SIDE, full)

    def take_left(u):
        left_copy(u).wait_recv()
        spread_left(u)

    def relay_left(u):
        row_copy(0, u).wait_recv()
        row_copy(1, u).wait_recv()
        relay_copy(u).start()
        pair_left_copy(SIDE + u).start()
        pair_left_copy(3 * SIDE + u).start()

    def end_left(t):
        relay_copy(t).wait_recv()
        pair_left_copy(2 * SIDE + t).start()

    ring(1)
    over(0, 2, lambda i: attend(0, 2 - 2 * i))
    over(1, SIDE, take_left)
    ring(2)
    for r in LATE:
        late_copy(r).wait_recv()
    attend(1, 2)

    wide_chunk = min(OUT_CHUNK, width)
    chunks = width // wide_chunk

    def cols_of(j):
        return pl.ds(pl.multiple_of(j * wide_chunk, HD), wide_chunk)

    def part_copy(d, j):
        here = part_out.at[pl.ds(d * half, half), cols_of(j)]
        there = part_in.at[pl.ds((1 - d) * half, half), cols_of(j)]
        return remote(
            here, there, part_send.at[d, j], part_recv.at[d, j], device(1 if d == 0 else SIDE - 1, 0)
        )

    def dot(a, b):
        return jnp.dot(a, b, preferred_element_type=jnp.float32)

    def product(at, cols):
        r = dot(attended[at, :depth], weight[0, :, cols])
        return r + dot(attended[at, depth:], weight[1, :left_row, cols])

    def project_sent(j):
        cols = cols_of(j)
        part_out[:, cols] = product(pl.ds(tile, tile), cols).astype(jnp.bfloat16)
        part_copy(0, j).start()
        part_copy(1, j).start()

    def project_kept(j):
        cols = cols_of(j)
        own[:, cols] = product(pl.ds(0, tile), cols)

    own_weight.wait()
    w_copy.wait_recv()
    mix_wait(0)
    over(0, chunks, project_sent)
    ring(3)
    attend(1, 0)
    over(0, SIDE, relay_left)
    ring(4)
    mix_wait(1)
    over(0, chunks, project_kept)
    over(0, SIDE, end_left)
    over(0, CHIPS, lambda i: pair_left_copy(i).wait_recv())
    attend_left()
    ring(5)
    over(1, SIDE, lambda dy: left_mix_copy(dy).wait_recv())

    @pl.when(core == 0)
    def _():
        over(0, clips, lambda origin: other_copy(origin).wait_recv())


    def finish(j):
        cols = cols_of(j)
        r = dot(left_attended[:, : 2 * HD], weight[1, left_row:, cols])
        r = r + dot(left_attended[:, 2 * HD :], other[:, cols])
        part_copy(0, j).wait_recv()
        part_copy(1, j).wait_recv()
        total = own[:, cols] + r + part_in[:, cols].astype(jnp.float32) + bias_ref[:, cols]
        out_ref[:, cols] = (gate_ref[:, cols] * total).astype(jnp.bfloat16)

    over(0, chunks, finish)

    over(1, SIDE, lambda dy: left_copy(dy).wait_send())
    for r in FAR:
        full_copy(r).wait_send()
    for r in LATE:
        late_copy(r).wait_send()
    over(0, CHIPS, lambda r: pair_copy(r).wait_send())

    def row_sent(t):
        row_copy(0, t).wait_send()
        row_copy(1, t).wait_send()
        relay_copy(t).wait_send()

    over(0, SIDE, row_sent)
    over(0, CHIPS, lambda i: pair_left_copy(i).wait_send())
    w_copy.wait_send()
    over(1, SIDE, lambda dy: left_mix_copy(dy).wait_send())

    @pl.when(core == 1)
    def _():
        near_copy(0).wait_send()
        near_copy(1).wait_send()
        for d in range(2):
            for step in range(1, ring_steps[d] + 1):
                ring_copy(d, step).wait_send()
        over(0, clips, lambda origin: other_copy(origin).wait_send())

    for rnd in range(2):

        def mix_sent(t, rnd=rnd):
            mix_copy(rnd, 2 * (t // SIDE), lax.rem(t, SIDE)).wait_send()

        over(1, 2 * SIDE, mix_sent)

    def sent(j):
        part_copy(0, j).wait_send()
        part_copy(1, j).wait_send()

    over(0, chunks, sent)


def body(q_in, k_in, v_in, q_gain, k_gain, out_weight, out_bias, out_gate):
    tile = q_in.shape[0]
    depth, width = out_weight.shape
    keys = 2 * CHIPS * tile
    chunks = width // min(OUT_CHUNK, width)
    clips = lax.axis_size("clip")
    vmem = pl.BlockSpec(memory_space=pltpu.VMEM)
    dma = pltpu.SemaphoreType.DMA
    return pl.pallas_call(
        kernel,
        out_shape=pltpu.VMEM((tile, width), jnp.bfloat16),
        in_specs=[vmem] * 5 + [pl.BlockSpec(memory_space=pl.ANY)] + [vmem] * 2,
        out_specs=vmem,
        scratch_shapes=[
            pltpu.VMEM((3, HEADS, tile, HD), jnp.bfloat16),
            pltpu.VMEM((2, 3, keys, HD), jnp.bfloat16),
            pltpu.VMEM((keys, SIDE * tile), jnp.float32),
            pltpu.VMEM((2, 2 * SIDE, tile, HD), jnp.bfloat16),
            pltpu.VMEM((2 * tile, 2 * SIDE * HD), jnp.bfloat16),
            pltpu.VMEM((SIDE, tile, HD), jnp.bfloat16),
            pltpu.VMEM((tile, SIDE * HD), jnp.bfloat16),
            pltpu.VMEM((2, depth, width), jnp.bfloat16),
            pltpu.VMEM((2 * HD, width), jnp.bfloat16),
            pltpu.VMEM((tile, width), jnp.float32),
            pltpu.VMEM((tile, width), jnp.bfloat16),
            pltpu.VMEM((tile, width), jnp.bfloat16),
            dma((3,)),
            dma((CHIPS,)), dma((CHIPS,)),
            dma((CHIPS,)), dma((CHIPS,)),
            dma((SIDE,)), dma((SIDE,)),
            dma((2, SIDE)), dma((2, SIDE)),
            dma((SIDE,)), dma((SIDE,)),
            dma((CHIPS,)), dma((CHIPS,)),
            dma((CHIPS,)), dma((CHIPS,)),
            dma, dma,
            dma((2,)), dma((2,)),
            dma((2, clips)), dma((2, clips)),
            dma((clips,)), dma((clips,)),
            dma((SIDE,)), dma((SIDE,)),
            dma((2, 2 * SIDE)), dma((2, 2 * SIDE)),
            dma((2, chunks)), dma((2, chunks)),
        ],
        compiler_params=pltpu.CompilerParams(
            collective_id=0, has_side_effects=True, vmem_limit_bytes=60 * 1024 * 1024
        ),
        name="attention_branch",
    )(
        q_in, k_in, v_in, q_gain, k_gain, out_weight,
        out_bias.reshape(1, -1), out_gate.reshape(1, -1),
    )


def solution(mesh):
    split = P(("clip", "blk", "head"), None)
    in_specs = (split, split, split, P(), P(), P("head", None), P(), P())
    return jax.shard_map(body, mesh=mesh, in_specs=in_specs, out_specs=split, check_vma=False)
```

```python
import functools
import math

import jax
import jax.numpy as jnp
from jax import lax
from jax.experimental import pallas as pl
from jax.experimental.pallas import tpu as pltpu
from jax.sharding import PartitionSpec as P

HD = 128
SIDE = 4
CHIPS = SIDE * SIDE
CLASS_HEADS = 10
HEADS = 20
KEY_CHUNK = 512
OUT_CHUNK = 1024
MESH = pl.DeviceIdType.MESH


def hops(r):
    dy, dx = r // SIDE, r % SIDE
    return min(dy, SIDE - dy) + min(dx, SIDE - dx)


FAR = sorted(range(1, CHIPS), key=lambda r: -hops(r))
LATE = [r for r in FAR if r // SIDE % 2 == 0]


def kernel(
    q_ref, k_ref, v_ref, qg_ref, kg_ref, w_ref, bias_ref, gate_ref, out_ref,
    stage, qkv, scores, mixed, attended, left_mixed, left_attended, weight, other, own, part_out, part_in,
    local_sem, go_sem, full_send, full_recv, late_send, late_recv, left_send, left_recv, row_send, row_recv, relay_send, relay_recv,
    pair_send, pair_recv, pair_left_send, pair_left_recv, w_send, w_recv,
    near_send, near_recv, ring_send, ring_recv, other_send, other_recv, left_mix_send, left_mix_recv,
    mix_send, mix_recv, part_send, part_recv,
):
    tile = q_ref.shape[0]
    half = tile // 2
    keys = 2 * CHIPS * tile
    width = out_ref.shape[1]
    blk, head, z = lax.axis_index("blk"), lax.axis_index("head"), lax.axis_index("clip")
    clips = lax.axis_size("clip")
    depth = w_ref.shape[0]
    left_row = 2 * SIDE * HD - depth
    piece = HD // clips
    x, core = lax.rem(blk, SIDE), lax.rem(head, 2)
    y = 2 * (blk // SIDE) + head // 2

    def chip(dy, dx):
        return lax.rem(y + dy, SIDE), lax.rem(x + dx, SIDE)

    def device(dy, dx):
        yy, xx = chip(dy, dx)
        return {"blk": (yy // 2) * SIDE + xx, "head": lax.rem(yy, 2) * 2 + core}

    sibling = {"blk": blk, "head": (head // 2) * 2 + 1 - core}

    def full_head(yy, xx):
        return CLASS_HEADS * lax.rem(yy, 2) + SIDE * (yy // 2) + xx

    def left_head(yy):
        return CLASS_HEADS * lax.rem(yy, 2) + 2 * SIDE + yy // 2

    def rows(start, size):
        return pl.ds(pl.multiple_of(start, half), size)

    def remote(src, dst, send, recv, target):
        return pltpu.make_async_remote_copy(
            src_ref=src, dst_ref=dst, send_sem=send, recv_sem=recv,
            device_id=target, device_id_type=MESH,
        )

    own_weight = pltpu.make_async_copy(w_ref, weight.at[core], local_sem.at[2])
    own_weight.start()

    barrier = pltpu.get_barrier_semaphore()

    def greet(r, carry):
        yy, xx = chip(r // SIDE, lax.rem(r, SIDE))
        first = {"blk": (yy // 2) * SIDE + xx, "head": lax.rem(yy, 2) * 2}
        pl.semaphore_signal(barrier, inc=1, device_id=first, device_id_type=MESH)
        return carry

    lax.fori_loop(1, CHIPS, greet, 0)
    beside = [2, clips - 2, 1, clips - 1]

    def clip_at(dz):
        return {"clip": lax.rem(z + dz, clips), "blk": blk, "head": head}

    @pl.when(core == 1)
    def _():
        pl.semaphore_signal(barrier, inc=1, device_id=sibling, device_id_type=MESH)
        for dz in beside:
            pl.semaphore_signal(barrier, inc=1, device_id=clip_at(dz), device_id_type=MESH)

    def normalize(ref, gain_ref, which, scale):
        wide = ref[...].astype(jnp.float32)
        factor = lax.rsqrt(jnp.mean(wide * wide, axis=-1, keepdims=True) + 1e-06)
        for h in range(HEADS):
            cols = slice(h * HD, (h + 1) * HD)
            gain = gain_ref[cols].reshape(1, HD)
            if scale is not None:
                gain = gain * scale
            stage[which, h] = (ref[:, cols].astype(jnp.float32) * factor * gain).astype(jnp.bfloat16)

    normalize(q_ref, qg_ref, 0, HD ** (-0.5) * math.log2(math.e))
    normalize(k_ref, kg_ref, 1, None)
    for h in range(HEADS):
        stage[2, h] = v_ref[:, h * HD : (h + 1) * HD].T

    @pl.when(core == 0)
    def _():
        pl.semaphore_wait(barrier, 2 * CHIPS - 1)
        pl.semaphore_signal(go_sem, inc=1, device_id=sibling, device_id_type=MESH)

    @pl.when(core == 1)
    def _():
        pl.semaphore_wait(go_sem, 1)


    w_copy = remote(w_ref, weight.at[core], w_send, w_recv, sibling)
    w_copy.start()

    def near_copy(d):
        start = z * 2 * piece + d * piece
        return remote(
            w_ref.at[pl.ds(pl.multiple_of(left_row + start, piece), piece)],
            other.at[pl.ds(pl.multiple_of(start, piece), piece)],
            near_send.at[d], near_recv.at[d], device(1 + 2 * d, 0),
        )

    def slice_of(origin):
        return other.at[pl.ds(pl.multiple_of(origin * 2 * piece, 2 * piece), 2 * piece)]

    def clip_of(dz):
        return lax.rem(z + dz, clips)

    def ring_copy(k):
        if k < 4:
            moved, dz = slice_of(z), beside[k]
        elif k < 6:
            moved, dz = slice_of(clip_of(beside[5 - k])), beside[k - 2]
        else:
            start = clip_of(beside[7 - k]) * 2 * piece + (k - 6) * piece
            moved, dz = other.at[pl.ds(pl.multiple_of(start, piece), piece)], beside[k - 6]
        return remote(moved, moved, ring_send.at[k], ring_recv.at[k], clip_at(dz))

    def other_copy(origin):
        return remote(
            slice_of(origin), slice_of(origin), other_send.at[origin], other_recv.at[origin], sibling
        )

    def ring(step):
        @pl.when(core == 1)
        def _():
            if step == 1:
                pl.semaphore_wait(barrier, len(beside))
                near_copy(0).wait_recv()
                near_copy(1).wait_recv()
                for k in range(4):
                    ring_copy(k).start()
                other_copy(z).start()
            elif step == 2:
                for k in range(4):
                    ring_copy(k).wait_recv()
                for k in range(4, 8):
                    ring_copy(k).start()
                for dz in beside:
                    other_copy(clip_of(dz)).start()
            else:
                for k in range(4, 8):
                    ring_copy(k).wait_recv()
                for dz in (3, 4, 5):
                    other_copy(clip_of(dz)).start()

    def left_copy(dy):
        yy, xx = chip(dy, 0)
        return remote(
            stage.at[:, left_head(yy)], qkv.at[1, :, rows(dy * tile, tile), :],
            left_send.at[dy], left_recv.at[dy], device(dy, 0),
        )

    def full_copy(r):
        dy, dx = r // SIDE, r % SIDE
        first = 1 if dy % 2 == 0 else 0
        return remote(
            stage.at[pl.ds(first, 3 - first), full_head(*chip(dy, dx))],
            qkv.at[0, pl.ds(first, 3 - first), rows(r * tile, tile), :],
            full_send.at[r], full_recv.at[r], device(dy, dx),
        )

    def late_copy(r):
        dy, dx = r // SIDE, r % SIDE
        return remote(
            stage.at[0, full_head(*chip(dy, dx))], qkv.at[0, 0, rows(r * tile, tile), :],
            late_send.at[r], late_recv.at[r], device(dy, dx),
        )

    def pair_copy(r):
        here = qkv.at[0, pl.ds(1, 2), rows(r * tile, tile), :]
        there = qkv.at[0, pl.ds(1, 2), rows((CHIPS + r) * tile, tile), :]
        return remote(here, there, pair_send.at[r], pair_recv.at[r], sibling)

    def left_rows(i):
        return qkv.at[1, pl.ds(1, 2), rows(i * tile, tile), :]

    def row_copy(d, t):
        dx = 1 + 2 * d
        return remote(
            left_rows(t), left_rows(dx * SIDE + t), row_send.at[d, t], row_recv.at[d, t], device(0, dx)
        )

    def relay_copy(t):
        dx = 1 + 2 * (t // 2)
        return remote(
            left_rows(dx * SIDE + t), left_rows(2 * SIDE + t), relay_send.at[t], relay_recv.at[t],
            device(0, dx),
        )

    def pair_left_copy(i):
        return remote(
            left_rows(i), left_rows(CHIPS + i), pair_left_send.at[i], pair_left_recv.at[i], sibling
        )

    def over(first, last, act):
        def step(i, carry):
            act(i)
            return carry

        lax.fori_loop(first, last, step, 0)

    @pl.when(core == 1)
    def _():
        near_copy(0).start()
        near_copy(1).start()

    for r in FAR:
        full_copy(r).start()
    over(1, SIDE, lambda dy: left_copy(dy).start())
    for r in LATE:
        late_copy(r).start()
    own_full = pltpu.make_async_copy(
        stage.at[:, full_head(y, x)], qkv.at[0, :, pl.ds(0, tile), :], local_sem.at[0]
    )
    own_left = pltpu.make_async_copy(
        stage.at[:, left_head(y)], qkv.at[1, :, pl.ds(0, tile), :], local_sem.at[1]
    )
    own_full.start()
    own_left.start()
    own_full.wait()
    own_left.wait()
    pair_copy(0).start()

    def pass_on(r):
        full_copy(r).wait_recv()
        pair_copy(r).start()

    for r in FAR:
        pass_on(r)

    def spread_left(t):
        row_copy(0, t).start()
        row_copy(1, t).start()
        pair_left_copy(t).start()

    spread_left(0)
    over(0, CHIPS, lambda r: pair_copy(r).wait_recv())

    def softmax_rows(which, q):
        count = q.shape[0]
        chunk = min(KEY_CHUNK, keys)
        highest = jnp.full((8, count), -jnp.inf, jnp.float32)
        for c in range(keys // chunk):
            s = lax.dot_general(
                qkv[which, 1, pl.ds(c * chunk, chunk), :], q, (((1,), (1,)), ((), ())),
                preferred_element_type=jnp.float32,
            )
            scores[c * chunk : (c + 1) * chunk, :] = s
            highest = jnp.maximum(highest, jnp.max(s.reshape(chunk // 8, 8, count), axis=0))
        top = jnp.max(highest, axis=0, keepdims=True)
        summed = jnp.zeros((8, count), jnp.float32)
        total = jnp.zeros((HD, count), jnp.float32)
        for c in range(keys // chunk):
            p = jnp.exp2(scores[c * chunk : (c + 1) * chunk, :] - top)
            summed = summed + jnp.sum(p.reshape(chunk // 8, 8, count), axis=0)
            values = jnp.concatenate(
                [qkv[which, 2, pl.ds(k * tile, tile), :] for k in range(c * chunk // tile, (c + 1) * chunk // tile)],
                axis=1,
            )
            total = total + jnp.dot(values, p.astype(jnp.bfloat16), preferred_element_type=jnp.float32)
        return (total / jnp.sum(summed, axis=0, keepdims=True)).T.astype(jnp.bfloat16)

    def lanes_of(slot):
        return pl.ds(pl.multiple_of(slot * HD, HD), HD)

    def mix_place(rnd):
        return pl.ds((1 - rnd) * tile, tile), lanes_of(SIDE * (y // 2) + x)

    def mix_copy(rnd, ey, dx):
        place, t = mix_place(rnd), (ey // 2) * SIDE + dx
        return remote(
            mixed.at[rnd, t], attended.at[place[0], place[1]], mix_send.at[rnd, t], mix_recv.at[rnd, t],
            device(ey, dx),
        )

    def attend(rnd, ey):
        pieces = []
        for dx in range(SIDE):

            def at(dy):
                return (lax.rem(dy, SIDE) * SIDE + (SIDE - dx) % SIDE) * tile

            if rnd == 0:
                pieces += [
                    qkv[0, 0, rows(at(2 * SIDE - ey - 1) + half, half), :],
                    qkv[0, 0, rows(at(2 * SIDE - ey + 1), half), :],
                ]
            else:
                pieces.append(qkv[0, 0, rows(at(2 * SIDE - ey), tile), :])
        result = softmax_rows(0, jnp.concatenate(pieces, axis=0))
        for dx in range(SIDE):
            mixed[rnd, (ey // 2) * SIDE + dx] = result[dx * tile : (dx + 1) * tile]

        @pl.when(ey == 0)
        def _():
            place = mix_place(rnd)
            attended[place[0], place[1]] = result[:tile]

        pl.when(ey > 0)(lambda: mix_copy(rnd, ey, 0).start())
        for dx in (2, 1, 3):
            mix_copy(rnd, ey, dx).start()

    def left_place(dy):
        return lanes_of(y // 2 + 2 * (dy & 1 if isinstance(dy, int) else lax.rem(dy, 2)))

    def left_mix_copy(dy):
        return remote(
            left_mixed.at[dy], left_attended.at[:, left_place(dy)], left_mix_send.at[dy],
            left_mix_recv.at[dy], device(SIDE - dy, 0),
        )

    def attend_left():
        result = softmax_rows(1, qkv[1, 0, pl.ds(0, SIDE * tile), :])
        left_attended[:, left_place(0)] = result[:tile]
        for dy in (2, 1, 3):
            left_mixed[dy] = result[dy * tile : (dy + 1) * tile]
            left_mix_copy(dy).start()

    def mix_wait(rnd):
        def full(t):
            mix_copy(rnd, 2 * (t // SIDE), lax.rem(t, SIDE)).wait_recv()

        over(1, 2 * SIDE, full)

    def take_left(u):
        left_copy(u).wait_recv()
        spread_left(u)

    def relay_left(u):
        row_copy(0, u).wait_recv()
        row_copy(1, u).wait_recv()
        relay_copy(u).start()
        pair_left_copy(SIDE + u).start()
        pair_left_copy(3 * SIDE + u).start()

    def end_left(t):
        relay_copy(t).wait_recv()
        pair_left_copy(2 * SIDE + t).start()

    ring(1)
    over(0, 2, lambda i: attend(0, 2 - 2 * i))
    over(1, SIDE, take_left)
    for r in LATE:
        late_copy(r).wait_recv()
    attend(1, 2)

    wide_chunk = min(OUT_CHUNK, width)
    chunks = width // wide_chunk

    def cols_of(j):
        return pl.ds(pl.multiple_of(j * wide_chunk, HD), wide_chunk)

    def part_copy(d, j):
        here = part_out.at[pl.ds(d * half, half), cols_of(j)]
        there = part_in.at[pl.ds((1 - d) * half, half), cols_of(j)]
        return remote(
            here, there, part_send.at[d, j], part_recv.at[d, j], device(1 if d == 0 else SIDE - 1, 0)
        )

    def dot(a, b):
        return jnp.dot(a, b, preferred_element_type=jnp.float32)

    def product(at, cols):
        r = dot(attended[at, :depth], weight[0, :, cols])
        return r + dot(attended[at, depth:], weight[1, :left_row, cols])

    def project_sent(j):
        cols = cols_of(j)
        part_out[:, cols] = product(pl.ds(tile, tile), cols).astype(jnp.bfloat16)
        part_copy(0, j).start()
        part_copy(1, j).start()

    def project_kept(j):
        cols = cols_of(j)
        own[:, cols] = product(pl.ds(0, tile), cols)

    own_weight.wait()
    w_copy.wait_recv()
    mix_wait(0)
    over(0, chunks, project_sent)
    attend(1, 0)
    over(0, SIDE, relay_left)
    ring(2)
    mix_wait(1)
    over(0, chunks, project_kept)
    over(0, SIDE, end_left)
    over(0, CHIPS, lambda i: pair_left_copy(i).wait_recv())
    attend_left()
    ring(3)
    over(1, SIDE, lambda dy: left_mix_copy(dy).wait_recv())

    @pl.when(core == 0)
    def _():
        over(0, clips, lambda origin: other_copy(origin).wait_recv())


    def finish(j):
        cols = cols_of(j)
        r = dot(left_attended[:, : 2 * HD], weight[1, left_row:, cols])
        r = r + dot(left_attended[:, 2 * HD :], other[:, cols])
        part_copy(0, j).wait_recv()
        part_copy(1, j).wait_recv()
        total = own[:, cols] + r + part_in[:, cols].astype(jnp.float32) + bias_ref[:, cols]
        out_ref[:, cols] = (gate_ref[:, cols] * total).astype(jnp.bfloat16)

    over(0, chunks, finish)

    over(1, SIDE, lambda dy: left_copy(dy).wait_send())
    for r in FAR:
        full_copy(r).wait_send()
    for r in LATE:
        late_copy(r).wait_send()
    over(0, CHIPS, lambda r: pair_copy(r).wait_send())

    def row_sent(t):
        row_copy(0, t).wait_send()
        row_copy(1, t).wait_send()
        relay_copy(t).wait_send()

    over(0, SIDE, row_sent)
    over(0, CHIPS, lambda i: pair_left_copy(i).wait_send())
    w_copy.wait_send()
    over(1, SIDE, lambda dy: left_mix_copy(dy).wait_send())

    @pl.when(core == 1)
    def _():
        near_copy(0).wait_send()
        near_copy(1).wait_send()
        for k in range(8):
            ring_copy(k).wait_send()
        over(0, clips, lambda origin: other_copy(origin).wait_send())

    for rnd in range(2):

        def mix_sent(t, rnd=rnd):
            mix_copy(rnd, 2 * (t // SIDE), lax.rem(t, SIDE)).wait_send()

        over(1, 2 * SIDE, mix_sent)

    def sent(j):
        part_copy(0, j).wait_send()
        part_copy(1, j).wait_send()

    over(0, chunks, sent)


def body(q_in, k_in, v_in, q_gain, k_gain, out_weight, out_bias, out_gate):
    tile = q_in.shape[0]
    depth, width = out_weight.shape
    keys = 2 * CHIPS * tile
    chunks = width // min(OUT_CHUNK, width)
    clips = lax.axis_size("clip")
    vmem = pl.BlockSpec(memory_space=pltpu.VMEM)
    dma = pltpu.SemaphoreType.DMA
    return pl.pallas_call(
        kernel,
        out_shape=pltpu.VMEM((tile, width), jnp.bfloat16),
        in_specs=[vmem] * 5 + [pl.BlockSpec(memory_space=pl.ANY)] + [vmem] * 2,
        out_specs=vmem,
        scratch_shapes=[
            pltpu.VMEM((3, HEADS, tile, HD), jnp.bfloat16),
            pltpu.VMEM((2, 3, keys, HD), jnp.bfloat16),
            pltpu.VMEM((keys, SIDE * tile), jnp.float32),
            pltpu.VMEM((2, 2 * SIDE, tile, HD), jnp.bfloat16),
            pltpu.VMEM((2 * tile, 2 * SIDE * HD), jnp.bfloat16),
            pltpu.VMEM((SIDE, tile, HD), jnp.bfloat16),
            pltpu.VMEM((tile, SIDE * HD), jnp.bfloat16),
            pltpu.VMEM((2, depth, width), jnp.bfloat16),
            pltpu.VMEM((2 * HD, width), jnp.bfloat16),
            pltpu.VMEM((tile, width), jnp.float32),
            pltpu.VMEM((tile, width), jnp.bfloat16),
            pltpu.VMEM((tile, width), jnp.bfloat16),
            dma((3,)),
            pltpu.SemaphoreType.REGULAR,
            dma((CHIPS,)), dma((CHIPS,)),
            dma((CHIPS,)), dma((CHIPS,)),
            dma((SIDE,)), dma((SIDE,)),
            dma((2, SIDE)), dma((2, SIDE)),
            dma((SIDE,)), dma((SIDE,)),
            dma((CHIPS,)), dma((CHIPS,)),
            dma((CHIPS,)), dma((CHIPS,)),
            dma, dma,
            dma((2,)), dma((2,)),
            dma((8,)), dma((8,)),
            dma((clips,)), dma((clips,)),
            dma((SIDE,)), dma((SIDE,)),
            dma((2, 2 * SIDE)), dma((2, 2 * SIDE)),
            dma((2, chunks)), dma((2, chunks)),
        ],
        compiler_params=pltpu.CompilerParams(
            collective_id=0, has_side_effects=True, vmem_limit_bytes=60 * 1024 * 1024
        ),
        name="attention_branch",
    )(
        q_in, k_in, v_in, q_gain, k_gain, out_weight,
        out_bias.reshape(1, -1), out_gate.reshape(1, -1),
    )


def solution(mesh):
    split = P(("clip", "blk", "head"), None)
    in_specs = (split, split, split, P(), P(), P("head", None), P(), P())
    return jax.shard_map(body, mesh=mesh, in_specs=in_specs, out_specs=split, check_vma=False)
```

```python
import functools
import math

import jax
import jax.numpy as jnp
from jax import lax
from jax.experimental import pallas as pl
from jax.experimental.pallas import tpu as pltpu
from jax.sharding import PartitionSpec as P

HD = 128
SIDE = 4
CHIPS = SIDE * SIDE
CLASS_HEADS = 10
HEADS = 20
KEY_CHUNK = 512
OUT_CHUNK = 1024
MESH = pl.DeviceIdType.MESH


def hops(r):
    dy, dx = r // SIDE, r % SIDE
    return min(dy, SIDE - dy) + min(dx, SIDE - dx)


FAR = sorted(range(1, CHIPS), key=lambda r: -hops(r))
LATE = [r for r in FAR if r // SIDE % 2 == 0]


def kernel(
    q_ref, k_ref, v_ref, qg_ref, kg_ref, w_ref, bias_ref, gate_ref, out_ref,
    stage, qkv, scores, mixed, attended, left_mixed, left_attended, weight, other, own, part_out, part_in,
    local_sem, go_sem, full_send, full_recv, late_send, late_recv, left_send, left_recv, row_send, row_recv, relay_send, relay_recv,
    pair_send, pair_recv, pair_left_send, pair_left_recv, w_send, w_recv,
    near_send, near_recv, ring_send, ring_recv, other_send, other_recv, left_mix_send, left_mix_recv,
    mix_send, mix_recv, part_send, part_recv,
):
    tile = q_ref.shape[0]
    half = tile // 2
    keys = 2 * CHIPS * tile
    width = out_ref.shape[1]
    blk, head, z = lax.axis_index("blk"), lax.axis_index("head"), lax.axis_index("clip")
    clips = lax.axis_size("clip")
    depth = w_ref.shape[0]
    left_row = 2 * SIDE * HD - depth
    piece = HD // clips
    x, core = lax.rem(blk, SIDE), lax.rem(head, 2)
    y = 2 * (blk // SIDE) + head // 2

    def chip(dy, dx):
        return lax.rem(y + dy, SIDE), lax.rem(x + dx, SIDE)

    def device(dy, dx):
        yy, xx = chip(dy, dx)
        return {"blk": (yy // 2) * SIDE + xx, "head": lax.rem(yy, 2) * 2 + core}

    sibling = {"blk": blk, "head": (head // 2) * 2 + 1 - core}

    def full_head(yy, xx):
        return CLASS_HEADS * lax.rem(yy, 2) + SIDE * (yy // 2) + xx

    def left_head(yy):
        return CLASS_HEADS * lax.rem(yy, 2) + 2 * SIDE + yy // 2

    def rows(start, size):
        return pl.ds(pl.multiple_of(start, half), size)

    def remote(src, dst, send, recv, target):
        return pltpu.make_async_remote_copy(
            src_ref=src, dst_ref=dst, send_sem=send, recv_sem=recv,
            device_id=target, device_id_type=MESH,
        )

    own_weight = pltpu.make_async_copy(w_ref, weight.at[core], local_sem.at[2])
    own_weight.start()

    barrier = pltpu.get_barrier_semaphore()

    def greet(r, carry):
        yy, xx = chip(r // SIDE, lax.rem(r, SIDE))
        first = {"blk": (yy // 2) * SIDE + xx, "head": lax.rem(yy, 2) * 2}
        pl.semaphore_signal(barrier, inc=1, device_id=first, device_id_type=MESH)
        return carry

    lax.fori_loop(1, CHIPS, greet, 0)
    beside = [2, clips - 2, 1, clips - 1]

    def clip_at(dz):
        return {"clip": lax.rem(z + dz, clips), "blk": blk, "head": head}

    @pl.when(core == 1)
    def _():
        pl.semaphore_signal(barrier, inc=1, device_id=sibling, device_id_type=MESH)
        for dz in beside:
            pl.semaphore_signal(barrier, inc=1, device_id=clip_at(dz), device_id_type=MESH)

    def normalize(ref, gain_ref, which, scale):
        wide = ref[...].astype(jnp.float32)
        factor = lax.rsqrt(jnp.mean(wide * wide, axis=-1, keepdims=True) + 1e-06)
        for h in range(HEADS):
            cols = slice(h * HD, (h + 1) * HD)
            gain = gain_ref[cols].reshape(1, HD)
            if scale is not None:
                gain = gain * scale
            stage[which, h] = (ref[:, cols].astype(jnp.float32) * factor * gain).astype(jnp.bfloat16)

    normalize(q_ref, qg_ref, 0, HD ** (-0.5) * math.log2(math.e))
    normalize(k_ref, kg_ref, 1, None)
    for h in range(HEADS):
        stage[2, h] = v_ref[:, h * HD : (h + 1) * HD].T

    @pl.when(core == 0)
    def _():
        pl.semaphore_wait(barrier, 2 * CHIPS - 1)
        pl.semaphore_signal(go_sem, inc=1, device_id=sibling, device_id_type=MESH)

    @pl.when(core == 1)
    def _():
        pl.semaphore_wait(go_sem, 1)


    w_copy = remote(w_ref, weight.at[core], w_send, w_recv, sibling)
    w_copy.start()

    def near_copy(d):
        start = z * 2 * piece + d * piece
        return remote(
            w_ref.at[pl.ds(pl.multiple_of(left_row + start, piece), piece)],
            other.at[pl.ds(pl.multiple_of(start, piece), piece)],
            near_send.at[d], near_recv.at[d], device(1 + 2 * d, 0),
        )

    def slice_of(origin):
        return other.at[pl.ds(pl.multiple_of(origin * 2 * piece, 2 * piece), 2 * piece)]

    def clip_of(dz):
        return lax.rem(z + dz, clips)

    def ring_copy(k):
        if k < 4:
            moved, dz = slice_of(z), beside[k]
        elif k < 6:
            moved, dz = slice_of(clip_of(beside[5 - k])), beside[k - 2]
        else:
            start = clip_of(beside[7 - k]) * 2 * piece + (k - 6) * piece
            moved, dz = other.at[pl.ds(pl.multiple_of(start, piece), piece)], beside[k - 6]
        return remote(moved, moved, ring_send.at[k], ring_recv.at[k], clip_at(dz))

    def other_copy(origin):
        return remote(
            slice_of(origin), slice_of(origin), other_send.at[origin], other_recv.at[origin], sibling
        )

    def ring(step):
        @pl.when(core == 1)
        def _():
            if step == 1:
                pl.semaphore_wait(barrier, len(beside))
                near_copy(0).wait_recv()
                near_copy(1).wait_recv()
                for k in range(4):
                    ring_copy(k).start()
                other_copy(z).start()
            elif step == 2:
                for k in range(4):
                    ring_copy(k).wait_recv()
                for k in range(4, 8):
                    ring_copy(k).start()
                for dz in beside:
                    other_copy(clip_of(dz)).start()
            else:
                for k in range(4, 8):
                    ring_copy(k).wait_recv()
                for dz in (3, 4, 5):
                    other_copy(clip_of(dz)).start()

    def left_copy(dy):
        yy, xx = chip(dy, 0)
        return remote(
            stage.at[:, left_head(yy)], qkv.at[1, :, rows(dy * tile, tile), :],
            left_send.at[dy], left_recv.at[dy], device(dy, 0),
        )

    def full_copy(r):
        dy, dx = r // SIDE, r % SIDE
        first = 1 if dy % 2 == 0 else 0
        return remote(
            stage.at[pl.ds(first, 3 - first), full_head(*chip(dy, dx))],
            qkv.at[0, pl.ds(first, 3 - first), rows(r * tile, tile), :],
            full_send.at[r], full_recv.at[r], device(dy, dx),
        )

    def late_copy(r):
        dy, dx = r // SIDE, r % SIDE
        return remote(
            stage.at[0, full_head(*chip(dy, dx))], qkv.at[0, 0, rows(r * tile, tile), :],
            late_send.at[r], late_recv.at[r], device(dy, dx),
        )

    def pair_copy(r):
        here = qkv.at[0, pl.ds(1, 2), rows(r * tile, tile), :]
        there = qkv.at[0, pl.ds(1, 2), rows((CHIPS + r) * tile, tile), :]
        return remote(here, there, pair_send.at[r], pair_recv.at[r], sibling)

    def left_rows(i):
        return qkv.at[1, pl.ds(1, 2), rows(i * tile, tile), :]

    def row_copy(d, t):
        dx = 1 + 2 * d
        return remote(
            left_rows(t), left_rows(dx * SIDE + t), row_send.at[d, t], row_recv.at[d, t], device(0, dx)
        )

    def relay_copy(t):
        dx = 1 + 2 * (t // 2)
        return remote(
            left_rows(dx * SIDE + t), left_rows(2 * SIDE + t), relay_send.at[t], relay_recv.at[t],
            device(0, dx),
        )

    def pair_left_copy(i):
        return remote(
            left_rows(i), left_rows(CHIPS + i), pair_left_send.at[i], pair_left_recv.at[i], sibling
        )

    def over(first, last, act):
        def step(i, carry):
            act(i)
            return carry

        lax.fori_loop(first, last, step, 0)

    @pl.when(core == 1)
    def _():
        near_copy(0).start()
        near_copy(1).start()

    for r in FAR:
        full_copy(r).start()
    over(1, SIDE, lambda dy: left_copy(dy).start())
    for r in LATE:
        late_copy(r).start()
    own_full = pltpu.make_async_copy(
        stage.at[:, full_head(y, x)], qkv.at[0, :, pl.ds(0, tile), :], local_sem.at[0]
    )
    own_left = pltpu.make_async_copy(
        stage.at[:, left_head(y)], qkv.at[1, :, pl.ds(0, tile), :], local_sem.at[1]
    )
    own_full.start()
    own_left.start()
    own_full.wait()
    own_left.wait()
    pair_copy(0).start()

    def pass_on(r):
        full_copy(r).wait_recv()
        pair_copy(r).start()

    for r in FAR:
        pass_on(r)

    def spread_left(t):
        row_copy(0, t).start()
        row_copy(1, t).start()
        pair_left_copy(t).start()

    spread_left(0)
    over(0, CHIPS, lambda r: pair_copy(r).wait_recv())

    def softmax_rows(which, q):
        count = q.shape[0]
        chunk = min(KEY_CHUNK, keys)
        highest = jnp.full((8, count), -jnp.inf, jnp.float32)
        for c in range(keys // chunk):
            s = lax.dot_general(
                qkv[which, 1, pl.ds(c * chunk, chunk), :], q, (((1,), (1,)), ((), ())),
                preferred_element_type=jnp.float32,
            )
            scores[c * chunk : (c + 1) * chunk, :] = s
            highest = jnp.maximum(highest, jnp.max(s.reshape(chunk // 8, 8, count), axis=0))
        top = jnp.max(highest, axis=0, keepdims=True)
        summed = jnp.zeros((8, count), jnp.float32)
        total = jnp.zeros((HD, count), jnp.float32)
        for c in range(keys // chunk):
            p = jnp.exp2(scores[c * chunk : (c + 1) * chunk, :] - top)
            summed = summed + jnp.sum(p.reshape(chunk // 8, 8, count), axis=0)
            values = jnp.concatenate(
                [qkv[which, 2, pl.ds(k * tile, tile), :] for k in range(c * chunk // tile, (c + 1) * chunk // tile)],
                axis=1,
            )
            total = total + jnp.dot(values, p.astype(jnp.bfloat16), preferred_element_type=jnp.float32)
        return (total / jnp.sum(summed, axis=0, keepdims=True)).T.astype(jnp.bfloat16)

    def lanes_of(slot):
        return pl.ds(pl.multiple_of(slot * HD, HD), HD)

    def mix_place(rnd):
        return pl.ds((1 - rnd) * tile, tile), lanes_of(SIDE * (y // 2) + x)

    def mix_copy(rnd, ey, dx):
        place, t = mix_place(rnd), (ey // 2) * SIDE + dx
        return remote(
            mixed.at[rnd, t], attended.at[place[0], place[1]], mix_send.at[rnd, t], mix_recv.at[rnd, t],
            device(ey, dx),
        )

    def attend(rnd, ey):
        pieces = []
        for dx in range(SIDE):

            def at(dy):
                return (lax.rem(dy, SIDE) * SIDE + (SIDE - dx) % SIDE) * tile

            if rnd == 0:
                pieces += [
                    qkv[0, 0, rows(at(2 * SIDE - ey - 1) + half, half), :],
                    qkv[0, 0, rows(at(2 * SIDE - ey + 1), half), :],
                ]
            else:
                pieces.append(qkv[0, 0, rows(at(2 * SIDE - ey), tile), :])
        result = softmax_rows(0, jnp.concatenate(pieces, axis=0))
        for dx in range(SIDE):
            mixed[rnd, (ey // 2) * SIDE + dx] = result[dx * tile : (dx + 1) * tile]

        @pl.when(ey == 0)
        def _():
            place = mix_place(rnd)
            attended[place[0], place[1]] = result[:tile]

        pl.when(ey > 0)(lambda: mix_copy(rnd, ey, 0).start())
        for dx in (2, 1, 3):
            mix_copy(rnd, ey, dx).start()

    def left_place(dy):
        return lanes_of(y // 2 + 2 * (dy & 1 if isinstance(dy, int) else lax.rem(dy, 2)))

    def left_mix_copy(dy):
        return remote(
            left_mixed.at[dy], left_attended.at[:, left_place(dy)], left_mix_send.at[dy],
            left_mix_recv.at[dy], device(SIDE - dy, 0),
        )

    def attend_left():
        result = softmax_rows(1, qkv[1, 0, pl.ds(0, SIDE * tile), :])
        left_attended[:, left_place(0)] = result[:tile]
        for dy in (2, 1, 3):
            left_mixed[dy] = result[dy * tile : (dy + 1) * tile]
            left_mix_copy(dy).start()

    def mix_wait(rnd):
        def full(t):
            mix_copy(rnd, 2 * (t // SIDE), lax.rem(t, SIDE)).wait_recv()

        over(1, 2 * SIDE, full)

    def take_left(u):
        left_copy(u).wait_recv()
        spread_left(u)

    def relay_left(u):
        row_copy(0, u).wait_recv()
        row_copy(1, u).wait_recv()
        relay_copy(u).start()
        pair_left_copy(SIDE + u).start()
        pair_left_copy(3 * SIDE + u).start()

    def end_left(t):
        relay_copy(t).wait_recv()
        pair_left_copy(2 * SIDE + t).start()

    ring(1)
    over(0, 2, lambda i: attend(0, 2 - 2 * i))
    over(1, SIDE, take_left)
    for r in LATE:
        late_copy(r).wait_recv()
    attend(1, 2)

    wide_chunk = min(OUT_CHUNK, width)
    chunks = width // wide_chunk

    def cols_of(j):
        return pl.ds(pl.multiple_of(j * wide_chunk, HD), wide_chunk)

    def part_copy(d, j):
        here = part_out.at[pl.ds(d * half, half), cols_of(j)]
        there = part_in.at[pl.ds((1 - d) * half, half), cols_of(j)]
        return remote(
            here, there, part_send.at[d, j], part_recv.at[d, j], device(1 if d == 0 else SIDE - 1, 0)
        )

    def dot(a, b):
        return jnp.dot(a, b, preferred_element_type=jnp.float32)

    def product(at, cols):
        r = dot(attended[at, :depth], weight[0, :, cols])
        return r + dot(attended[at, depth:], weight[1, :left_row, cols])

    def project_sent(j):
        cols = cols_of(j)
        part_out[:, cols] = product(pl.ds(tile, tile), cols).astype(jnp.bfloat16)
        part_copy(0, j).start()
        part_copy(1, j).start()

    def project_kept(j):
        cols = cols_of(j)
        own[:, cols] = product(pl.ds(0, tile), cols)

    own_weight.wait()
    w_copy.wait_recv()
    mix_wait(0)
    over(0, chunks, project_sent)
    attend(1, 0)
    over(0, SIDE, relay_left)
    ring(2)
    over(0, SIDE, end_left)
    over(0, CHIPS, lambda i: pair_left_copy(i).wait_recv())
    attend_left()
    mix_wait(1)
    over(0, chunks, project_kept)
    ring(3)
    over(1, SIDE, lambda dy: left_mix_copy(dy).wait_recv())

    @pl.when(core == 0)
    def _():
        over(0, clips, lambda origin: other_copy(origin).wait_recv())


    def finish(j):
        cols = cols_of(j)
        r = dot(left_attended[:, : 2 * HD], weight[1, left_row:, cols])
        r = r + dot(left_attended[:, 2 * HD :], other[:, cols])
        part_copy(0, j).wait_recv()
        part_copy(1, j).wait_recv()
        total = own[:, cols] + r + part_in[:, cols].astype(jnp.float32) + bias_ref[:, cols]
        out_ref[:, cols] = (gate_ref[:, cols] * total).astype(jnp.bfloat16)

    over(0, chunks, finish)

    over(1, SIDE, lambda dy: left_copy(dy).wait_send())
    for r in FAR:
        full_copy(r).wait_send()
    for r in LATE:
        late_copy(r).wait_send()
    over(0, CHIPS, lambda r: pair_copy(r).wait_send())

    def row_sent(t):
        row_copy(0, t).wait_send()
        row_copy(1, t).wait_send()
        relay_copy(t).wait_send()

    over(0, SIDE, row_sent)
    over(0, CHIPS, lambda i: pair_left_copy(i).wait_send())
    w_copy.wait_send()
    over(1, SIDE, lambda dy: left_mix_copy(dy).wait_send())

    @pl.when(core == 1)
    def _():
        near_copy(0).wait_send()
        near_copy(1).wait_send()
        for k in range(8):
            ring_copy(k).wait_send()
        over(0, clips, lambda origin: other_copy(origin).wait_send())

    for rnd in range(2):

        def mix_sent(t, rnd=rnd):
            mix_copy(rnd, 2 * (t // SIDE), lax.rem(t, SIDE)).wait_send()

        over(1, 2 * SIDE, mix_sent)

    def sent(j):
        part_copy(0, j).wait_send()
        part_copy(1, j).wait_send()

    over(0, chunks, sent)


def body(q_in, k_in, v_in, q_gain, k_gain, out_weight, out_bias, out_gate):
    tile = q_in.shape[0]
    depth, width = out_weight.shape
    keys = 2 * CHIPS * tile
    chunks = width // min(OUT_CHUNK, width)
    clips = lax.axis_size("clip")
    vmem = pl.BlockSpec(memory_space=pltpu.VMEM)
    dma = pltpu.SemaphoreType.DMA
    return pl.pallas_call(
        kernel,
        out_shape=pltpu.VMEM((tile, width), jnp.bfloat16),
        in_specs=[vmem] * 5 + [pl.BlockSpec(memory_space=pl.ANY)] + [vmem] * 2,
        out_specs=vmem,
        scratch_shapes=[
            pltpu.VMEM((3, HEADS, tile, HD), jnp.bfloat16),
            pltpu.VMEM((2, 3, keys, HD), jnp.bfloat16),
            pltpu.VMEM((keys, SIDE * tile), jnp.float32),
            pltpu.VMEM((2, 2 * SIDE, tile, HD), jnp.bfloat16),
            pltpu.VMEM((2 * tile, 2 * SIDE * HD), jnp.bfloat16),
            pltpu.VMEM((SIDE, tile, HD), jnp.bfloat16),
            pltpu.VMEM((tile, SIDE * HD), jnp.bfloat16),
            pltpu.VMEM((2, depth, width), jnp.bfloat16),
            pltpu.VMEM((2 * HD, width), jnp.bfloat16),
            pltpu.VMEM((tile, width), jnp.float32),
            pltpu.VMEM((tile, width), jnp.bfloat16),
            pltpu.VMEM((tile, width), jnp.bfloat16),
            dma((3,)),
            pltpu.SemaphoreType.REGULAR,
            dma((CHIPS,)), dma((CHIPS,)),
            dma((CHIPS,)), dma((CHIPS,)),
            dma((SIDE,)), dma((SIDE,)),
            dma((2, SIDE)), dma((2, SIDE)),
            dma((SIDE,)), dma((SIDE,)),
            dma((CHIPS,)), dma((CHIPS,)),
            dma((CHIPS,)), dma((CHIPS,)),
            dma, dma,
            dma((2,)), dma((2,)),
            dma((8,)), dma((8,)),
            dma((clips,)), dma((clips,)),
            dma((SIDE,)), dma((SIDE,)),
            dma((2, 2 * SIDE)), dma((2, 2 * SIDE)),
            dma((2, chunks)), dma((2, chunks)),
        ],
        compiler_params=pltpu.CompilerParams(
            collective_id=0, has_side_effects=True, vmem_limit_bytes=60 * 1024 * 1024
        ),
        name="attention_branch",
    )(
        q_in, k_in, v_in, q_gain, k_gain, out_weight,
        out_bias.reshape(1, -1), out_gate.reshape(1, -1),
    )


def solution(mesh):
    split = P(("clip", "blk", "head"), None)
    in_specs = (split, split, split, P(), P(), P("head", None), P(), P())
    return jax.shard_map(body, mesh=mesh, in_specs=in_specs, out_specs=split, check_vma=False)
```
